512 devices in a mesh: section: 4 (over y_hi), seq: 32 (over z, y_lo, core), exp: 4 (over x).
Axes of the slice: x: 4, y: 8 (y_hi: 4, y_lo: 2; y = y_hi * 2 + y_lo), z: 8, core: 2. Of those that a mesh axis runs over, the one named last changes fastest.
Arguments:
- latent: bfloat16 [8, 128, 64, 384], P('section', 'seq', 'exp'), may hold values from -6 to 6
- cotangent: bfloat16 [8, 128, 64, 384], P('section', 'seq', 'exp'), may hold values from -6 to 6
- gain_one: float32 [384], replicated, may hold values from 0.5 to 2
- gain_two: float32 [384], replicated, may hold values from 0.5 to 2
- kernel_one: bfloat16 [3, 3, 3, 384, 384], P(None, None, None, 'exp'), may hold values from -0.0625 to 0.0625
- kernel_two: bfloat16 [3, 3, 3, 384, 384], P(None, None, None, 'exp'), may hold values from -0.0625 to 0.0625
Outputs:
- block_out: bfloat16 [8, 128, 64, 384], P('section', 'seq', 'exp')
- latent_grad: bfloat16 [8, 128, 64, 384], P('section', 'seq', 'exp')
The draws below stay inside these ranges and needn't reach their ends.
All inputs are finite; a program needn't handle non-finite values.
Results may differ from the reference program's by a relative error of at most 0.015.
Values may be sent and summed in bfloat16 or wider, within the bound.
No kernel may reach another device: no remote copies, remote signals or barrier semaphores. Data moves between devices by JAX's collectives and lax.ppermute only.
A program may use at most 64 MiB of HBM per device.

```python
import math
import jax
import jax.numpy as jnp
from jax import lax

C = 384
NT = 8
NH = 128
NW = 64


def block_levels(rng, shape, pieces, least, top_value):
    loudness, own = 1.0, jax.random.fold_in(rng, 6)
    for position, parts in pieces:
        draws = jnp.exp(jax.random.uniform(jax.random.fold_in(own, position), (parts,), jnp.float32, least / len(pieces), top_value / len(pieces)))
        loudness = loudness * jnp.repeat(draws, shape[position] // parts).reshape([-1 if axis == position else 1 for axis in range(len(shape))])
    return loudness


def bell_draw(rng, shape, spread, limit, pieces=(), kind=jnp.bfloat16):
    loudness = block_levels(rng, shape, pieces, -0.22, 0.18) if pieces else 1.0
    array = jax.random.normal(rng, shape, jnp.float32) * spread * loudness
    return jnp.minimum(jnp.maximum(array, -limit), limit).astype(kind)


def setup_inputs(seed: int = 0) -> dict:
    keys = jax.random.split(jax.random.key(seed), 7)
    return {
        "latent": bell_draw(keys[0], (NT, NH, NW, C), 1.0, 6.0, ((0, 4), (1, 32), (2, 4))),
        "cotangent": bell_draw(keys[1], (NT, NH, NW, C), 1.0, 6.0, ((0, 4), (1, 32), (2, 4))),
        "gain_one": jnp.clip(jnp.exp(jax.random.uniform(keys[2], (C,), jnp.float32, math.log(0.5), math.log(2.0))), 0.5, 2.0),
        "gain_two": jnp.clip(jnp.exp(jax.random.uniform(keys[3], (C,), jnp.float32, math.log(0.5), math.log(2.0))), 0.5, 2.0),
        "kernel_one": bell_draw(keys[4], (3, 3, 3, C, C), (27 * C) ** -0.5, 0.0625, ((3, 4),)),
        "kernel_two": bell_draw(keys[5], (3, 3, 3, C, C), (27 * C) ** -0.5, 0.0625, ((3, 4),)),
    }


epsilon = 1e-06

def normalize(values, gain):
    inverse = lax.rsqrt(lax.optimization_barrier(jnp.mean(values * values, axis=-1, keepdims=True)) + epsilon)
    return (values * inverse * gain, inverse)

def norm_backward(values, inverse, gain, upstream):
    scaled = upstream * gain
    return inverse * scaled - values * inverse ** 3 * lax.optimization_barrier(jnp.mean(values * scaled, axis=-1, keepdims=True))

def silu_slope(normed):
    sigma = jax.nn.sigmoid(normed)
    return sigma * (1.0 + normed * (1.0 - sigma))

def forward_kernel(weight):
    swapped = jnp.swapaxes(weight, 3, 4)
    return swapped.reshape(3, 3, 3 * swapped.shape[3], swapped.shape[4])

def backward_kernel(weight):
    flipped = weight[::-1, ::-1, ::-1]
    return flipped.reshape(3, 3, 3 * flipped.shape[3], flipped.shape[4])

def conv_taps(padded, kernel, frame_count, row_count, col_count):
    summed = jnp.zeros((frame_count * row_count * col_count, kernel.shape[3]), jnp.float32)
    for time_tap in range(3):
        for row_tap in range(3):
            columns = jnp.concatenate([padded[time_tap:time_tap + frame_count, row_tap:row_tap + row_count, col_tap:col_tap + col_count] for col_tap in range(3)], axis=-1)
            columns = columns.reshape(frame_count * row_count * col_count, columns.shape[-1])
            summed = summed + jnp.dot(columns, kernel[time_tap, row_tap], preferred_element_type=jnp.float32)
    return summed.reshape(frame_count, row_count, col_count, kernel.shape[3])

def conv_whole(padded, kernel):

    def one_frame(index):
        window = lax.dynamic_slice_in_dim(padded, index, 3, 0)
        return conv_taps(window, kernel, 1, NH, NW)[0]
    return lax.map(one_frame, jnp.arange(NT, dtype=jnp.int32))

def reference(latent, cotangent, gain_one, gain_two, kernel_one, kernel_two):
    ahead = ((2, 0), (1, 1), (1, 1), (0, 0))
    behind = ((0, 2), (1, 1), (1, 1), (0, 0))
    source = latent.astype(jnp.float32)
    normed_one, inverse_one = normalize(source, gain_one)
    active_one = jax.nn.silu(normed_one).astype(jnp.bfloat16)
    inner = conv_whole(jnp.pad(active_one, ahead), forward_kernel(kernel_one))
    normed_two, inverse_two = normalize(inner, gain_two)
    active_two = jax.nn.silu(normed_two).astype(jnp.bfloat16)
    branch = conv_whole(jnp.pad(active_two, ahead), forward_kernel(kernel_two))
    block_out = (source + branch).astype(jnp.bfloat16)
    grad_two = conv_whole(jnp.pad(cotangent, behind), backward_kernel(kernel_two))
    grad_inner = norm_backward(inner, inverse_two, gain_two, grad_two * silu_slope(normed_two)).astype(jnp.bfloat16)
    grad_one = conv_whole(jnp.pad(grad_inner, behind), backward_kernel(kernel_one))
    latent_grad = cotangent.astype(jnp.float32) + norm_backward(source, inverse_one, gain_one, grad_one * silu_slope(normed_one))
    return (block_out, latent_grad.astype(jnp.bfloat16))
```

```python
import functools
import jax
import jax.numpy as jnp
from jax import lax
from jax.experimental import pallas as pl
from jax.experimental.pallas import tpu as pltpu
from jax.sharding import PartitionSpec as P

epsilon = 1e-06
F32 = jnp.float32
BF16 = jnp.bfloat16

T, H, W, C, O, X = 2, 4, 16, 384, 96, 4
WT, WH = T + 2, H + 2
COLS = X * W
LANES = 128
DATA = WT * WH
SENT = DATA + WH
BACK = T * H + T


def vmem(count):
    return [pl.BlockSpec(memory_space=pltpu.VMEM)] * count


def call(kernel, out_shape, *operands, scratch=(), scalars=0, flops=0):
    bytes_accessed = sum(a.size * a.dtype.itemsize for a in operands)
    outs = out_shape if isinstance(out_shape, (list, tuple)) else [out_shape]
    bytes_accessed += sum(a.size * a.dtype.itemsize for a in outs)
    smem = [pl.BlockSpec(memory_space=pltpu.SMEM)] * scalars
    return pl.pallas_call(
        kernel,
        out_shape=out_shape,
        in_specs=smem + vmem(len(operands) - scalars),
        out_specs=vmem(len(outs)) if isinstance(out_shape, (list, tuple)) else vmem(1)[0],
        scratch_shapes=list(scratch),
        compiler_params=pltpu.CompilerParams(vmem_limit_bytes=40 * 1024 * 1024),
        cost_estimate=pl.CostEstimate(
            flops=flops, bytes_accessed=bytes_accessed, transcendentals=0
        ),
    )(*operands)


def sigmoid(values):
    return 1.0 / (1.0 + jnp.exp(-values))


def normalize(values, gain):
    inverse = lax.rsqrt(jnp.mean(values * values, axis=-1, keepdims=True) + epsilon)
    return values * inverse * gain, inverse


def norm_backward(values, inverse, gain, upstream):
    scaled = upstream * gain
    return inverse * scaled - values * inverse**3 * jnp.mean(
        values * scaled, axis=-1, keepdims=True
    )


def silu_slope(normed):
    sigma = sigmoid(normed)
    return sigma * (1.0 + normed * (1.0 - sigma))


def put_data(out, frame, row, block):
    for target in range(X):
        out[target, frame * WH + row] = block


def put_slices(out, row, blocks):
    for target in range(X):
        out[target, DATA + row] = jnp.concatenate(
            [block[:, target * O : (target + 1) * O] for block in blocks], axis=-1
        )


def pack_one_kernel(gain, own, before, lat_row, lat_corner, cot, cot_after, cot_row, cot_corner, out):
    scale = gain[...]

    def active(block):
        normed, _ = normalize(block.astype(F32), scale)
        return (normed * sigmoid(normed)).astype(BF16)

    for frame in range(T):
        for row in range(H):
            put_data(out, frame, row, active(before[frame, row]))
            put_data(out, T + frame, row, active(own[frame, row]))
        for row in range(2):
            put_data(out, frame, H + row, active(lat_corner[frame, row]))
            put_data(out, T + frame, H + row, active(lat_row[frame, row]))
    for row in range(H):
        put_slices(out, row, [cot[0, row], cot[1, row], cot_after[0, row], cot_after[1, row]])
    for row in range(2):
        put_slices(
            out,
            H + row,
            [cot_row[0, row], cot_row[1, row], cot_corner[0, row], cot_corner[1, row]],
        )


def pack_two_kernel(own, before, act_row, act_corner, grad, grad_after, grad_row, grad_corner, out):
    for frame in range(T):
        for row in range(2):
            put_data(out, frame, row, act_corner[frame, row])
            put_data(out, T + frame, row, act_row[frame, row])
        for row in range(H):
            put_data(out, frame, 2 + row, before[frame, row])
            put_data(out, T + frame, 2 + row, own[frame, row])
    for row in range(2):
        put_slices(
            out,
            row,
            [grad_row[0, row], grad_row[1, row], grad_corner[0, row], grad_corner[1, row]],
        )
    for row in range(H):
        put_slices(
            out, 2 + row, [grad[0, row], grad[1, row], grad_after[0, row], grad_after[1, row]]
        )


def shifted_sum(parts):
    size = parts[0].shape[0]
    column = lax.broadcasted_iota(jnp.int32, (size, 1), 0) % COLS
    low = jnp.where(column == 0, 0.0, pltpu.roll(parts[0], 1, 0))
    high = jnp.where(column == COLS - 1, 0.0, pltpu.roll(parts[2], size - 1, 0))
    return low + parts[1] + high


def conv_kernel(flags, got, ahead_weight, back_weight, out, data, grads):
    taps = (
        ((0, 0), (1, None), (2, None), (3, 1)),
        ((1, None), (2, None), (3, None), (4, None)),
        ((2, None), (3, None), (4, 2), (5, 3)),
    )
    zeros = jnp.zeros((W, LANES - O), BF16)
    for tap, reads in enumerate(taps):
        for row, (source, flag) in enumerate(reads):
            for part in range(X):
                place = slice(row * COLS + part * W, row * COLS + (part + 1) * W)
                for frame in range(WT):
                    block = got[part, frame * WH + source]
                    if flag is not None:
                        block = block * flags[flag].astype(BF16)
                    data[frame, place, tap * C : (tap + 1) * C] = block
                block = got[part, DATA + source]
                if flag is not None:
                    block = block * flags[flag].astype(BF16)
                for frame in range(WT):
                    piece = jnp.concatenate([block[:, frame * O : (frame + 1) * O], zeros], axis=-1)
                    grads[frame, place, tap * LANES : (tap + 1) * LANES] = piece
    size = T * H * COLS
    total = jnp.zeros((size, 3 * O), F32)
    for time_tap in range(3):
        total = total + lax.dot_general(
            data[time_tap : time_tap + T].reshape(size, 3 * C),
            jnp.concatenate(
                [ahead_weight[time_tap, tap].reshape(3 * O, C) for tap in range(3)], axis=-1
            ),
            (((1,), (1,)), ((), ())),
            preferred_element_type=F32,
        )
    result = shifted_sum([total[:, tap * O : (tap + 1) * O] for tap in range(3)])
    result = result.astype(BF16)
    for frame in range(T):
        for target in range(X):
            start = [(frame * H + row) * COLS + target * W for row in range(H)]
            out[target, T * H + frame] = jnp.concatenate(
                [result[at : at + W] for at in start], axis=-1
            )
    total = jnp.zeros((size, 3 * C), F32)
    for time_tap in range(3):
        total = total + jnp.dot(
            grads[time_tap : time_tap + T].reshape(size, 3 * LANES),
            back_weight[time_tap],
            preferred_element_type=F32,
        )
    result = shifted_sum([total[:, tap * C : (tap + 1) * C] for tap in range(3)]).astype(BF16)
    for block in range(T * H):
        for target in range(X):
            at = block * COLS + target * W
            out[target, block] = result[at : at + W]


def arrived_grad(got, block):
    total = got[0, block].astype(F32)
    for source in range(1, X):
        total = total + got[source, block].astype(F32)
    return total


def arrived_conv(got, frame, row):
    return jnp.concatenate(
        [got[source, T * H + frame, :, row * O : (row + 1) * O] for source in range(X)], axis=-1
    ).astype(F32)


def middle_kernel(gain, got, active, grad_inner):
    scale = gain[...]
    for frame in range(T):
        for row in range(H):
            inner = arrived_conv(got, frame, row)
            grad_two = arrived_grad(got, frame * H + row)
            normed, inverse = normalize(inner, scale)
            active[frame, row] = (normed * sigmoid(normed)).astype(BF16)
            grad_inner[frame, row] = norm_backward(
                inner, inverse, scale, grad_two * silu_slope(normed)
            ).astype(BF16)


def last_kernel(gain, latent, cotangent, got, block_out, latent_grad):
    scale = gain[...]
    for frame in range(T):
        for row in range(H):
            source = latent[frame, row].astype(F32)
            block_out[frame, row] = (source + arrived_conv(got, frame, row)).astype(BF16)
            normed, inverse = normalize(source, scale)
            grad_one = arrived_grad(got, frame * H + row)
            latent_grad[frame, row] = (
                cotangent[frame, row].astype(F32)
                + norm_backward(source, inverse, scale, grad_one * silu_slope(normed))
            ).astype(BF16)


def shift(values, frames, rows):
    sections, ring = lax.axis_size("section"), lax.axis_size("seq")
    pairs = [
        (s * ring + q, (s + frames) * ring + (q + rows) % ring)
        for s in range(sections)
        for q in range(ring)
        if 0 <= s + frames < sections
    ]
    return lax.ppermute(values, ("section", "seq"), pairs)


def exchange(values):
    return lax.all_to_all(values, "exp", split_axis=0, concat_axis=0, tiled=True)


def back_weight_kernel(weight, out):
    zeros = jnp.zeros((LANES - O, 3 * C), BF16)
    for time_tap in range(3):
        for row_tap in range(3):
            start = row_tap * LANES
            for tap in range(3):
                out[time_tap, start : start + O, tap * C : (tap + 1) * C] = weight[
                    2 - time_tap, 2 - row_tap, 2 - tap
                ]
            out[time_tap, start + O : start + LANES] = zeros


def back_kernel(weight):
    shape = jax.ShapeDtypeStruct((3, 3 * LANES, 3 * C), BF16)
    return call(back_weight_kernel, shape, weight)


def convs(flags, got, ahead_weight, back_weight):
    size = T * H * COLS
    return call(
        conv_kernel,
        jax.ShapeDtypeStruct((X, BACK, W, C), BF16),
        flags,
        got,
        ahead_weight,
        back_weight,
        scratch=(
            pltpu.VMEM((WT, H * COLS, 3 * C), BF16),
            pltpu.VMEM((WT, H * COLS, 3 * LANES), BF16),
        ),
        scalars=1,
        flops=2 * size * 27 * 2 * C * LANES,
    )


def body(latent, cotangent, gain_one, gain_two, kernel_one, kernel_two):
    gain_one, gain_two = gain_one.reshape(1, C), gain_two.reshape(1, C)
    place, last = lax.axis_index("seq"), lax.axis_size("seq") - 1
    one = jnp.ones((), F32)
    not_first, not_last = (place != 0).astype(F32), (place != last).astype(F32)
    flags_one = jnp.stack([one, not_last, not_last, one])
    flags_two = jnp.stack([not_first, one, one, not_last])
    block = jax.ShapeDtypeStruct((T, H, W, C), BF16)
    sent = jax.ShapeDtypeStruct((X, SENT, W, C), BF16)

    before = shift(latent, 1, 0)
    after = shift(cotangent, -1, 0)
    rows = shift(jnp.stack([latent[:, :2], cotangent[:, :2]]), 0, -1)
    lat_corner = shift(latent[:, :2], 1, -1)
    cot_corner = shift(cotangent[:, :2], -1, -1)
    packed = call(
        pack_one_kernel,
        sent,
        gain_one,
        latent,
        before,
        rows[0],
        lat_corner,
        cotangent,
        after,
        rows[1],
        cot_corner,
    )
    got = exchange(packed)
    summed = convs(flags_one, got, kernel_one, back_kernel(kernel_two))
    got = exchange(summed)
    active, grad_inner = call(middle_kernel, [block, block], gain_two, got)

    before = shift(active, 1, 0)
    after = shift(grad_inner, -1, 0)
    rows = shift(jnp.stack([active[:, 2:], grad_inner[:, 2:]]), 0, 1)
    act_corner = shift(active[:, 2:], 1, 1)
    grad_corner = shift(grad_inner[:, 2:], -1, 1)
    packed = call(
        pack_two_kernel,
        sent,
        active,
        before,
        rows[0],
        act_corner,
        grad_inner,
        after,
        rows[1],
        grad_corner,
    )
    got = exchange(packed)
    summed = convs(flags_two, got, kernel_two, back_kernel(kernel_one))
    got = exchange(summed)
    return tuple(call(last_kernel, [block, block], gain_one, latent, cotangent, got))


def solution(mesh):
    in_specs = (
        P("section", "seq", "exp", None),
        P("section", "seq", "exp", None),
        P(),
        P(),
        P(None, None, None, "exp", None),
        P(None, None, None, "exp", None),
    )
    out_specs = (P("section", "seq", "exp", None), P("section", "seq", "exp", None))
    return jax.shard_map(body, mesh=mesh, in_specs=in_specs, out_specs=out_specs, check_vma=False)
```

```python
import jax
import jax.numpy as jnp
from jax import lax
from jax.experimental import pallas as pl
from jax.experimental.pallas import tpu as pltpu
from jax.sharding import PartitionSpec as P

epsilon = 1e-06
F32 = jnp.float32
BF16 = jnp.bfloat16

T, H, W, C, O, X = 2, 4, 16, 384, 96, 4
WT = T + 2
SIZE = T * H * W * X
COLS = X * W
LANES = 128
KINDS = WT + 1
BACK = T * H + T


def vmem(count):
    return [pl.BlockSpec(memory_space=pltpu.VMEM)] * count


def call(kernel, out_shape, *operands, scratch=(), flops=0):
    bytes_accessed = sum(a.size * a.dtype.itemsize for a in operands)
    outs = out_shape if isinstance(out_shape, (list, tuple)) else [out_shape]
    bytes_accessed += sum(a.size * a.dtype.itemsize for a in outs)
    return pl.pallas_call(
        kernel,
        out_shape=out_shape,
        in_specs=vmem(len(operands)),
        out_specs=vmem(len(outs)) if isinstance(out_shape, (list, tuple)) else vmem(1)[0],
        scratch_shapes=list(scratch),
        compiler_params=pltpu.CompilerParams(vmem_limit_bytes=40 * 1024 * 1024),
        cost_estimate=pl.CostEstimate(
            flops=flops, bytes_accessed=bytes_accessed, transcendentals=0
        ),
    )(*operands)


def sigmoid(values):
    return 1.0 / (1.0 + jnp.exp(-values))


def normalize(values, gain):
    inverse = lax.rsqrt(jnp.mean(values * values, axis=-1, keepdims=True) + epsilon)
    return values * inverse * gain, inverse


def norm_backward(values, inverse, gain, upstream):
    scaled = upstream * gain
    return inverse * scaled - values * inverse**3 * jnp.mean(
        values * scaled, axis=-1, keepdims=True
    )


def silu_slope(normed):
    sigma = sigmoid(normed)
    return sigma * (1.0 + normed * (1.0 - sigma))


def put_slices(out, row, blocks):
    for target in range(X):
        out[target, row, WT] = jnp.concatenate(
            [block[:, target * O : (target + 1) * O] for block in blocks], axis=-1
        )


def pack_one_kernel(gain, own, before, cot, after, out):
    scale = gain[...]
    for row in range(H):
        for frame in range(WT):
            block = before[frame, row] if frame < 2 else own[frame - 2, row]
            normed, _ = normalize(block.astype(F32), scale)
            block = (normed * sigmoid(normed)).astype(BF16)
            for target in range(X):
                out[target, row, frame] = block
        put_slices(out, row, [cot[0, row], cot[1, row], after[0, row], after[1, row]])


def pack_two_kernel(own, before, grad, after, out):
    for row in range(H):
        for frame in range(WT):
            block = before[frame, row] if frame < 2 else own[frame - 2, row]
            for target in range(X):
                out[target, row, frame] = block
        put_slices(out, row, [grad[0, row], grad[1, row], after[0, row], after[1, row]])


def shifted_sum(parts):
    size = parts[0].shape[0]
    column = lax.broadcasted_iota(jnp.int32, (size, 1), 0) % COLS
    low = jnp.where(column == 0, 0.0, pltpu.roll(parts[0], 1, 0))
    high = jnp.where(column == COLS - 1, 0.0, pltpu.roll(parts[2], size - 1, 0))
    return low + parts[1] + high


def ahead_dot(values, weight):
    return lax.dot_general(
        values, weight, (((1,), (1,)), ((), ())), preferred_element_type=F32
    )


def padded_slice(block, frame):
    zeros = jnp.zeros((W, LANES - O), BF16)
    return jnp.concatenate([block[:, frame * O : (frame + 1) * O], zeros], axis=-1)


def conv_kernel(got, ahead_weight, back_weight, ahead_out, back_out, data, grads):
    for row in range(H):
        for part in range(X):
            block = got[part, row, WT]
            pieces = [padded_slice(block, frame) for frame in range(WT)]
            for tap in range(3):
                target = row + 1 - tap
                if 0 <= target < H:
                    place = slice(target * COLS + part * W, target * COLS + (part + 1) * W)
                    for frame in range(WT):
                        data[frame, place, tap * C : (tap + 1) * C] = got[part, row, frame]
                        grads[frame, place, tap * LANES : (tap + 1) * LANES] = pieces[frame]
    for tap, row in ((0, 0), (2, H - 1)):
        place = slice(row * COLS, (row + 1) * COLS)
        for frame in range(WT):
            data[frame, place, tap * C : (tap + 1) * C] = jnp.zeros((COLS, C), BF16)
            grads[frame, place, tap * LANES : (tap + 1) * LANES] = jnp.zeros((COLS, LANES), BF16)
    total = jnp.zeros((SIZE, 3 * O), F32)
    for time_tap in range(3):
        total = total + ahead_dot(
            data[time_tap : time_tap + T].reshape(SIZE, 3 * C), ahead_weight[time_tap]
        )
    ahead_out[...] = shifted_sum([total[:, tap * O : (tap + 1) * O] for tap in range(3)])
    total = jnp.zeros((SIZE, 3 * C), F32)
    for time_tap in range(3):
        total = total + jnp.dot(
            grads[time_tap : time_tap + T].reshape(SIZE, 3 * LANES),
            back_weight[time_tap],
            preferred_element_type=F32,
        )
    back_out[...] = shifted_sum([total[:, tap * C : (tap + 1) * C] for tap in range(3)])


def edge_kernel(up, down, ahead_weight, back_weight, ahead, back, out, data, grads):
    ahead_parts, back_parts = [], []
    for side, rows in enumerate((up, down)):
        for part in range(X):
            place = slice(part * W, (part + 1) * W)
            for frame in range(WT):
                data[side, frame, place] = rows[part, frame]
                grads[side, frame, place] = padded_slice(rows[part, WT], frame)
        tap = 2 * side
        ahead_total = jnp.zeros((T * COLS, 3 * O), F32)
        back_total = jnp.zeros((T * COLS, 3 * C), F32)
        for time_tap in range(3):
            ahead_total = ahead_total + ahead_dot(
                data[side, time_tap : time_tap + T].reshape(T * COLS, C),
                ahead_weight[time_tap, :, tap * C : (tap + 1) * C],
            )
            back_total = back_total + jnp.dot(
                grads[side, time_tap : time_tap + T].reshape(T * COLS, LANES),
                back_weight[time_tap, tap * LANES : (tap + 1) * LANES],
                preferred_element_type=F32,
            )
        ahead_parts.append(shifted_sum([ahead_total[:, k * O : (k + 1) * O] for k in range(3)]))
        back_parts.append(shifted_sum([back_total[:, k * C : (k + 1) * C] for k in range(3)]))
    for frame in range(T):
        rows = []
        for row in range(H):
            start = (frame * H + row) * COLS
            ahead_row = ahead[start : start + COLS]
            back_row = back[start : start + COLS]
            if row in (0, H - 1):
                side, at = row // (H - 1), frame * COLS
                ahead_row = ahead_row + ahead_parts[side][at : at + COLS]
                back_row = back_row + back_parts[side][at : at + COLS]
            rows.append(ahead_row.astype(BF16))
            back_row = back_row.astype(BF16)
            for target in range(X):
                out[target, frame * H + row] = back_row[target * W : (target + 1) * W]
        rows = jnp.concatenate(rows, axis=-1)
        for target in range(X):
            out[target, T * H + frame] = rows[target * W : (target + 1) * W]


def arrived_grad(got, block):
    total = got[0, block].astype(F32)
    for source in range(1, X):
        total = total + got[source, block].astype(F32)
    return total


def arrived_conv(got, frame, row):
    return jnp.concatenate(
        [got[source, T * H + frame, :, row * O : (row + 1) * O] for source in range(X)], axis=-1
    ).astype(F32)


def middle_kernel(gain, got, active, grad_inner):
    scale = gain[...]
    for frame in range(T):
        for row in range(H):
            inner = arrived_conv(got, frame, row)
            grad_two = arrived_grad(got, frame * H + row)
            normed, inverse = normalize(inner, scale)
            active[frame, row] = (normed * sigmoid(normed)).astype(BF16)
            grad_inner[frame, row] = norm_backward(
                inner, inverse, scale, grad_two * silu_slope(normed)
            ).astype(BF16)


def last_kernel(gain, latent, cotangent, got, block_out, latent_grad):
    scale = gain[...]
    for frame in range(T):
        for row in range(H):
            source = latent[frame, row].astype(F32)
            block_out[frame, row] = (source + arrived_conv(got, frame, row)).astype(BF16)
            normed, inverse = normalize(source, scale)
            grad_one = arrived_grad(got, frame * H + row)
            latent_grad[frame, row] = (
                cotangent[frame, row].astype(F32)
                + norm_backward(source, inverse, scale, grad_one * silu_slope(normed))
            ).astype(BF16)


def shift(values, axis, by):
    size = lax.axis_size(axis)
    pairs = [(i, i + by) for i in range(size) if 0 <= i + by < size]
    return lax.ppermute(values, axis, pairs)


def exchange(values):
    return lax.all_to_all(values, "exp", split_axis=0, concat_axis=0, tiled=True)


def weights_kernel(ahead, back, ahead_out, back_out):
    zeros = jnp.zeros((LANES - O, 3 * C), BF16)
    for time_tap in range(3):
        for row_tap in range(3):
            start = row_tap * LANES
            for tap in range(3):
                ahead_out[
                    time_tap, tap * O : (tap + 1) * O, row_tap * C : (row_tap + 1) * C
                ] = ahead[time_tap, row_tap, tap]
                back_out[time_tap, start : start + O, tap * C : (tap + 1) * C] = back[
                    2 - time_tap, 2 - row_tap, 2 - tap
                ]
            back_out[time_tap, start + O : start + LANES] = zeros


def weights(ahead, back):
    shapes = [
        jax.ShapeDtypeStruct((3, 3 * O, 3 * C), BF16),
        jax.ShapeDtypeStruct((3, 3 * LANES, 3 * C), BF16),
    ]
    return call(weights_kernel, shapes, ahead, back)


def convs(packed, ahead, back):
    got = exchange(packed)
    ahead_weight, back_weight = weights(ahead, back)
    up = shift(got[:, H - 1], "seq", 1)
    down = shift(got[:, 0], "seq", -1)
    sums = call(
        conv_kernel,
        [jax.ShapeDtypeStruct((SIZE, O), F32), jax.ShapeDtypeStruct((SIZE, C), F32)],
        got,
        ahead_weight,
        back_weight,
        scratch=(
            pltpu.VMEM((WT, H * COLS, 3 * C), BF16),
            pltpu.VMEM((WT, H * COLS, 3 * LANES), BF16),
        ),
        flops=2 * SIZE * 27 * 2 * C * LANES,
    )
    summed = call(
        edge_kernel,
        jax.ShapeDtypeStruct((X, BACK, W, C), BF16),
        up,
        down,
        ahead_weight,
        back_weight,
        *sums,
        scratch=(
            pltpu.VMEM((2, WT, COLS, C), BF16),
            pltpu.VMEM((2, WT, COLS, LANES), BF16),
        ),
        flops=SIZE * 9 * 2 * C * LANES,
    )
    return exchange(summed)


def body(latent, cotangent, gain_one, gain_two, kernel_one, kernel_two):
    gain_one, gain_two = gain_one.reshape(1, C), gain_two.reshape(1, C)
    block = jax.ShapeDtypeStruct((T, H, W, C), BF16)
    sent = jax.ShapeDtypeStruct((X, H, KINDS, W, C), BF16)

    before = shift(latent, "section", 1)
    after = shift(cotangent, "section", -1)
    packed = call(pack_one_kernel, sent, gain_one, latent, before, cotangent, after)
    got = convs(packed, kernel_one, kernel_two)
    active, grad_inner = call(middle_kernel, [block, block], gain_two, got)

    before = shift(active, "section", 1)
    after = shift(grad_inner, "section", -1)
    packed = call(pack_two_kernel, sent, active, before, grad_inner, after)
    got = convs(packed, kernel_two, kernel_one)
    return tuple(call(last_kernel, [block, block], gain_one, latent, cotangent, got))


def solution(mesh):
    in_specs = (
        P("section", "seq", "exp", None),
        P("section", "seq", "exp", None),
        P(),
        P(),
        P(None, None, None, "exp", None),
        P(None, None, None, "exp", None),
    )
    out_specs = (P("section", "seq", "exp", None), P("section", "seq", "exp", None))
    return jax.shard_map(body, mesh=mesh, in_specs=in_specs, out_specs=out_specs, check_vma=False)
```

```python
import jax
import jax.numpy as jnp
from jax import lax
from jax.experimental import pallas as pl
from jax.experimental.pallas import tpu as pltpu
from jax.sharding import PartitionSpec as P

epsilon = 1e-06
F32 = jnp.float32
BF16 = jnp.bfloat16

T, H, W, C, O, X = 2, 4, 16, 384, 96, 4
WT = T + 2
SIZE = T * H * W * X
COLS = X * W
LANES = 128
KINDS = WT + 1
BACK = T * H + T


def places(count, space):
    return [pl.BlockSpec(memory_space=space)] * count


def call(kernel, out_shape, *operands, scratch=(), flops=0, far=0):
    bytes_accessed = sum(a.size * a.dtype.itemsize for a in operands)
    outs = out_shape if isinstance(out_shape, (list, tuple)) else [out_shape]
    bytes_accessed += sum(a.size * a.dtype.itemsize for a in outs)
    near = len(operands) - far
    pinned = [pltpu.with_memory_space_constraint(a, pltpu.HBM) for a in operands[near:]]
    return pl.pallas_call(
        kernel,
        out_shape=out_shape,
        in_specs=places(near, pltpu.VMEM) + places(far, pltpu.HBM),
        out_specs=places(len(outs), pltpu.VMEM) if outs is out_shape else places(1, pltpu.VMEM)[0],
        scratch_shapes=list(scratch),
        compiler_params=pltpu.CompilerParams(vmem_limit_bytes=40 * 1024 * 1024),
        cost_estimate=pl.CostEstimate(
            flops=flops, bytes_accessed=bytes_accessed, transcendentals=0
        ),
    )(*operands[:near], *pinned)


def sigmoid(values):
    return 1.0 / (1.0 + jnp.exp(-values))


def normalize(values, gain):
    inverse = lax.rsqrt(jnp.mean(values * values, axis=-1, keepdims=True) + epsilon)
    return values * inverse * gain, inverse


def norm_backward(values, inverse, gain, upstream):
    scaled = upstream * gain
    return inverse * scaled - values * inverse**3 * jnp.mean(
        values * scaled, axis=-1, keepdims=True
    )


def silu_slope(normed):
    sigma = sigmoid(normed)
    return sigma * (1.0 + normed * (1.0 - sigma))


def put_slices(out, row, blocks):
    for target in range(X):
        out[target, row, WT] = jnp.concatenate(
            [block[:, target * O : (target + 1) * O] for block in blocks], axis=-1
        )


def put_active(out, row, frame, block, scale):
    normed, _ = normalize(block.astype(F32), scale)
    block = (normed * sigmoid(normed)).astype(BF16)
    for target in range(X):
        out[target, row, frame] = block


def pack_one_kernel(gain, before, after, own_far, cot_far, out, own, cot, sems):
    scale = gain[...]
    copies = [
        pltpu.make_async_copy(own_far, own, sems.at[0]),
        pltpu.make_async_copy(cot_far, cot, sems.at[1]),
    ]
    for copy in copies:
        copy.start()
    for row in range(H):
        for frame in range(T):
            put_active(out, row, frame, before[frame, row], scale)
    copies[0].wait()
    for row in range(H):
        for frame in range(T):
            put_active(out, row, T + frame, own[frame, row], scale)
    copies[1].wait()
    for row in range(H):
        put_slices(out, row, [cot[0, row], cot[1, row], after[0, row], after[1, row]])


def pack_two_kernel(own, before, grad, after, out):
    for row in range(H):
        for frame in range(WT):
            block = before[frame, row] if frame < 2 else own[frame - 2, row]
            for target in range(X):
                out[target, row, frame] = block
        put_slices(out, row, [grad[0, row], grad[1, row], after[0, row], after[1, row]])


def shifted_sum(parts):
    size = parts[0].shape[0]
    column = lax.broadcasted_iota(jnp.int32, (size, 1), 0) % COLS
    low = jnp.where(column == 0, 0.0, pltpu.roll(parts[0], 1, 0))
    high = jnp.where(column == COLS - 1, 0.0, pltpu.roll(parts[2], size - 1, 0))
    return low + parts[1] + high


def ahead_dot(values, weight):
    return lax.dot_general(
        values, weight, (((1,), (1,)), ((), ())), preferred_element_type=F32
    )


def padded_slice(block, frame):
    zeros = jnp.zeros((W, LANES - O), BF16)
    return jnp.concatenate([block[:, frame * O : (frame + 1) * O], zeros], axis=-1)


def own_taps():
    return [
        (tap, row, row + 1 - tap) for tap in range(3) for row in range(H) if 0 <= row + 1 - tap < H
    ]


def clear_borders(operand, width):
    for tap, row in ((0, 0), (2, H - 1)):
        place = slice(row * COLS, (row + 1) * COLS)
        for frame in range(WT):
            operand[frame, place, tap * width : (tap + 1) * width] = jnp.zeros((COLS, width), BF16)


def ahead_kernel(got, weight, out, data):
    for tap, row, target in own_taps():
        for part in range(X):
            place = slice(target * COLS + part * W, target * COLS + (part + 1) * W)
            for frame in range(WT):
                data[frame, place, tap * C : (tap + 1) * C] = got[part, row, frame]
    clear_borders(data, C)
    total = jnp.zeros((3 * O, SIZE), F32)
    for time_tap in range(3):
        total = total + ahead_dot(
            weight[time_tap], data[time_tap : time_tap + T].reshape(SIZE, 3 * C)
        )
    column = lax.broadcasted_iota(jnp.int32, (1, SIZE), 1) % COLS
    low = jnp.where(column == 0, 0.0, pltpu.roll(total[:O], 1, 1))
    high = jnp.where(column == COLS - 1, 0.0, pltpu.roll(total[2 * O :], SIZE - 1, 1))
    out[...] = (low + total[O : 2 * O] + high).T


def back_kernel(got, weight, out, grads):
    for row in range(H):
        for part in range(X):
            block = got[part, row, WT]
            pieces = [padded_slice(block, frame) for frame in range(WT)]
            for tap, source, target in own_taps():
                if source == row:
                    place = slice(target * COLS + part * W, target * COLS + (part + 1) * W)
                    for frame in range(WT):
                        grads[frame, place, tap * LANES : (tap + 1) * LANES] = pieces[frame]
    clear_borders(grads, LANES)
    operand = jnp.concatenate(
        [grads[tap : tap + T].reshape(SIZE, 3 * LANES) for tap in range(3)], axis=-1
    )
    total = jnp.dot(
        operand, weight[...].reshape(9 * LANES, 3 * C), preferred_element_type=F32
    )
    out[...] = shifted_sum([total[:, tap * C : (tap + 1) * C] for tap in range(3)])


def edge_kernel(up, down, ahead_weight, back_weight, ahead, back, out, data, grads):
    ahead_parts, back_parts = [], []
    for side, rows in enumerate((up, down)):
        for part in range(X):
            place = slice(part * W, (part + 1) * W)
            for frame in range(WT):
                data[side, frame, place] = rows[part, frame]
                grads[side, frame, place] = padded_slice(rows[part, WT], frame)
        tap = 2 * side
        ahead_total = jnp.zeros((T * COLS, 3 * O), F32)
        back_total = jnp.zeros((T * COLS, 3 * C), F32)
        for time_tap in range(3):
            ahead_total = ahead_total + ahead_dot(
                data[side, time_tap : time_tap + T].reshape(T * COLS, C),
                ahead_weight[time_tap, :, tap * C : (tap + 1) * C],
            )
            back_total = back_total + jnp.dot(
                grads[side, time_tap : time_tap + T].reshape(T * COLS, LANES),
                back_weight[time_tap, tap * LANES : (tap + 1) * LANES],
                preferred_element_type=F32,
            )
        ahead_parts.append(shifted_sum([ahead_total[:, k * O : (k + 1) * O] for k in range(3)]))
        back_parts.append(shifted_sum([back_total[:, k * C : (k + 1) * C] for k in range(3)]))
    for frame in range(T):
        rows = []
        for row in range(H):
            start = (frame * H + row) * COLS
            ahead_row = ahead[start : start + COLS]
            back_row = back[start : start + COLS]
            if row in (0, H - 1):
                side, at = row // (H - 1), frame * COLS
                ahead_row = ahead_row + ahead_parts[side][at : at + COLS]
                back_row = back_row + back_parts[side][at : at + COLS]
            rows.append(ahead_row.astype(BF16))
            back_row = back_row.astype(BF16)
            for target in range(X):
                out[target, frame * H + row] = back_row[target * W : (target + 1) * W]
        rows = jnp.concatenate(rows, axis=-1)
        for target in range(X):
            out[target, T * H + frame] = rows[target * W : (target + 1) * W]


def arrived_grad(got, block):
    total = got[0, block].astype(F32)
    for source in range(1, X):
        total = total + got[source, block].astype(F32)
    return total


def arrived_conv(got, frame, row):
    return jnp.concatenate(
        [got[source, T * H + frame, :, row * O : (row + 1) * O] for source in range(X)], axis=-1
    ).astype(F32)


def middle_kernel(gain, got, active, grad_inner):
    scale = gain[...]
    for frame in range(T):
        for row in range(H):
            inner = arrived_conv(got, frame, row)
            grad_two = arrived_grad(got, frame * H + row)
            normed, inverse = normalize(inner, scale)
            active[frame, row] = (normed * sigmoid(normed)).astype(BF16)
            grad_inner[frame, row] = norm_backward(
                inner, inverse, scale, grad_two * silu_slope(normed)
            ).astype(BF16)


def last_kernel(gain, latent, cotangent, got, block_out, latent_grad):
    scale = gain[...]
    for frame in range(T):
        for row in range(H):
            source = latent[frame, row].astype(F32)
            block_out[frame, row] = (source + arrived_conv(got, frame, row)).astype(BF16)
            normed, inverse = normalize(source, scale)
            grad_one = arrived_grad(got, frame * H + row)
            latent_grad[frame, row] = (
                cotangent[frame, row].astype(F32)
                + norm_backward(source, inverse, scale, grad_one * silu_slope(normed))
            ).astype(BF16)


def shift(values, axis, by):
    size = lax.axis_size(axis)
    pairs = [(i, i + by) for i in range(size) if 0 <= i + by < size]
    return lax.ppermute(values, axis, pairs)


def exchange(values):
    return lax.all_to_all(values, "exp", split_axis=0, concat_axis=0, tiled=True)


def weights_kernel(ahead, back, ahead_out, back_out):
    zeros = jnp.zeros((LANES - O, 3 * C), BF16)
    for time_tap in range(3):
        for row_tap in range(3):
            start = row_tap * LANES
            for tap in range(3):
                ahead_out[
                    time_tap, tap * O : (tap + 1) * O, row_tap * C : (row_tap + 1) * C
                ] = ahead[time_tap, row_tap, tap]
                back_out[time_tap, start : start + O, tap * C : (tap + 1) * C] = back[
                    2 - time_tap, 2 - row_tap, 2 - tap
                ]
            back_out[time_tap, start + O : start + LANES] = zeros


WEIGHTS = [
    jax.ShapeDtypeStruct((3, 3 * O, 3 * C), BF16),
    jax.ShapeDtypeStruct((3, 3 * LANES, 3 * C), BF16),
]


def convs(packed, ahead, back):
    got = exchange(packed)
    ahead_weight, back_weight = call(weights_kernel, WEIGHTS, ahead, back)
    up = shift(got[:, H - 1], "seq", 1)
    down = shift(got[:, 0], "seq", -1)
    own_ahead = call(
        ahead_kernel,
        jax.ShapeDtypeStruct((SIZE, O), F32),
        got,
        ahead_weight,
        scratch=(pltpu.VMEM((WT, H * COLS, 3 * C), BF16),),
        flops=2 * SIZE * 27 * C * LANES,
    )
    own_back = call(
        back_kernel,
        jax.ShapeDtypeStruct((SIZE, C), F32),
        got,
        back_weight,
        scratch=(pltpu.VMEM((WT, H * COLS, 3 * LANES), BF16),),
        flops=2 * SIZE * 27 * C * LANES,
    )
    summed = call(
        edge_kernel,
        jax.ShapeDtypeStruct((X, BACK, W, C), BF16),
        up,
        down,
        ahead_weight,
        back_weight,
        own_ahead,
        own_back,
        scratch=(
            pltpu.VMEM((2, WT, COLS, C), BF16),
            pltpu.VMEM((2, WT, COLS, LANES), BF16),
        ),
        flops=SIZE * 9 * 2 * C * LANES,
    )
    return exchange(summed)


def body(latent, cotangent, gain_one, gain_two, kernel_one, kernel_two):
    gain_one, gain_two = gain_one.reshape(1, C), gain_two.reshape(1, C)
    block = jax.ShapeDtypeStruct((T, H, W, C), BF16)
    sent = jax.ShapeDtypeStruct((X, H, KINDS, W, C), BF16)

    before = shift(latent, "section", 1)
    after = shift(cotangent, "section", -1)
    packed = call(
        pack_one_kernel,
        sent,
        gain_one,
        before,
        after,
        latent,
        cotangent,
        scratch=(
            pltpu.VMEM((T, H, W, C), BF16),
            pltpu.VMEM((T, H, W, C), BF16),
            pltpu.SemaphoreType.DMA((2,)),
        ),
        far=2,
    )
    got = convs(packed, kernel_one, kernel_two)
    active, grad_inner = call(middle_kernel, [block, block], gain_two, got)

    before = shift(active, "section", 1)
    after = shift(grad_inner, "section", -1)
    packed = call(pack_two_kernel, sent, active, before, grad_inner, after)
    got = convs(packed, kernel_two, kernel_one)
    return tuple(call(last_kernel, [block, block], gain_one, latent, cotangent, got))


def solution(mesh):
    in_specs = (
        P("section", "seq", "exp", None),
        P("section", "seq", "exp", None),
        P(),
        P(),
        P(None, None, None, "exp", None),
        P(None, None, None, "exp", None),
    )
    out_specs = (P("section", "seq", "exp", None), P("section", "seq", "exp", None))
    return jax.shard_map(body, mesh=mesh, in_specs=in_specs, out_specs=out_specs, check_vma=False)
```

```python
import functools
import jax
import jax.numpy as jnp
from jax import lax
from jax.experimental import pallas as pl
from jax.experimental.pallas import tpu as pltpu
from jax.sharding import PartitionSpec as P

epsilon = 1e-06
F32 = jnp.float32
BF16 = jnp.bfloat16

T, H, W, C, O, X = 2, 4, 16, 384, 96, 4
WT = T + 2
SIZE = T * H * W * X
COLS = X * W
LANES = 128
KINDS = WT + 1
BACK = T * H + T


def places(count, space):
    return [pl.BlockSpec(memory_space=space)] * count


def call(kernel, out_shape, *operands, scratch=(), flops=0, far=0, far_out=False):
    bytes_accessed = sum(a.size * a.dtype.itemsize for a in operands)
    outs = out_shape if isinstance(out_shape, (list, tuple)) else [out_shape]
    bytes_accessed += sum(a.size * a.dtype.itemsize for a in outs)
    near = len(operands) - far
    out_specs = places(len(outs), pltpu.VMEM) if outs is out_shape else places(1, pltpu.VMEM)[0]
    if far_out:
        out_shape = pltpu.HBM(out_shape.shape, out_shape.dtype)
        out_specs = pl.BlockSpec(memory_space=pltpu.HBM)
    pinned = [pltpu.with_memory_space_constraint(a, pltpu.HBM) for a in operands[near:]]
    return pl.pallas_call(
        kernel,
        out_shape=out_shape,
        in_specs=places(near, pltpu.VMEM) + places(far, pltpu.HBM),
        out_specs=out_specs,
        scratch_shapes=list(scratch),
        compiler_params=pltpu.CompilerParams(vmem_limit_bytes=40 * 1024 * 1024),
        cost_estimate=pl.CostEstimate(
            flops=flops, bytes_accessed=bytes_accessed, transcendentals=0
        ),
    )(*operands[:near], *pinned)


def sigmoid(values):
    return 1.0 / (1.0 + jnp.exp(-values))


def normalize(values, gain):
    inverse = lax.rsqrt(jnp.mean(values * values, axis=-1, keepdims=True) + epsilon)
    return values * inverse * gain, inverse


def norm_backward(values, inverse, gain, upstream):
    scaled = upstream * gain
    return inverse * scaled - values * inverse**3 * jnp.mean(
        values * scaled, axis=-1, keepdims=True
    )


def silu_slope(normed):
    sigma = sigmoid(normed)
    return sigma * (1.0 + normed * (1.0 - sigma))


def put_slices(out, row, blocks):
    for target in range(X):
        out[target, row, WT] = jnp.concatenate(
            [block[:, target * O : (target + 1) * O] for block in blocks], axis=-1
        )


def activated(block, scale):
    normed, _ = normalize(block.astype(F32), scale)
    return (normed * sigmoid(normed)).astype(BF16)


def put_block(out, row, frame, block):
    for target in range(X):
        out[target, row, frame] = block


def own_kernel(gains, own_far, cot_far, active, cot, own, sems):
    copies = [
        pltpu.make_async_copy(own_far, own, sems.at[0]),
        pltpu.make_async_copy(cot_far, cot, sems.at[1]),
    ]
    for copy in copies:
        copy.start()
    copies[0].wait()
    scale = gains[0:1]
    for row in range(H):
        for frame in range(T):
            active[frame, row] = activated(own[frame, row], scale)
    copies[1].wait()


def pack_kernel(gains, before, own, cot, after, out_far, out, sems):
    copies = []
    for row in range(H):
        for frame in range(T):
            block = before[frame, row]
            put_block(out, row, frame, block if gains is None else activated(block, gains[0:1]))
            put_block(out, row, T + frame, own[frame, row])
        put_slices(out, row, [cot[0, row], cot[1, row], after[0, row], after[1, row]])
        copies.append(pltpu.make_async_copy(out.at[:, row], out_far.at[:, row], sems.at[row]))
        copies[row].start()
    for copy in copies:
        copy.wait()


def pack(kernel, *operands):
    sent = jax.ShapeDtypeStruct((X, H, KINDS, W, C), BF16)
    scratch = (pltpu.VMEM(sent.shape, BF16), pltpu.SemaphoreType.DMA((H,)))
    return call(kernel, sent, *operands, scratch=scratch, far_out=True)


def shifted_sum(parts):
    size = parts[0].shape[0]
    column = lax.broadcasted_iota(jnp.int32, (size, 1), 0) % COLS
    low = jnp.where(column == 0, 0.0, pltpu.roll(parts[0], 1, 0))
    high = jnp.where(column == COLS - 1, 0.0, pltpu.roll(parts[2], size - 1, 0))
    return low + parts[1] + high


def ahead_dot(values, weight):
    return lax.dot_general(
        values, weight, (((1,), (1,)), ((), ())), preferred_element_type=F32
    )


def padded_slice(block, frame):
    zeros = jnp.zeros((W, LANES - O), BF16)
    return jnp.concatenate([block[:, frame * O : (frame + 1) * O], zeros], axis=-1)


def own_taps():
    return [
        (tap, row, row + 1 - tap) for tap in range(3) for row in range(H) if 0 <= row + 1 - tap < H
    ]


def clear_borders(operand, width):
    for tap, row in ((0, 0), (2, H - 1)):
        place = slice(row * COLS, (row + 1) * COLS)
        for frame in range(WT):
            operand[frame, place, tap * width : (tap + 1) * width] = jnp.zeros((COLS, width), BF16)


def ahead_kernel(got, weight, out, data):
    for tap, row, target in own_taps():
        for part in range(X):
            place = slice(target * COLS + part * W, target * COLS + (part + 1) * W)
            for frame in range(WT):
                data[frame, place, tap * C : (tap + 1) * C] = got[part, row, frame]
    clear_borders(data, C)
    total = jnp.zeros((3 * O, SIZE), F32)
    for time_tap in range(3):
        total = total + ahead_dot(
            weight[time_tap], data[time_tap : time_tap + T].reshape(SIZE, 3 * C)
        )
    column = lax.broadcasted_iota(jnp.int32, (1, SIZE), 1) % COLS
    low = jnp.where(column == 0, 0.0, pltpu.roll(total[:O], 1, 1))
    high = jnp.where(column == COLS - 1, 0.0, pltpu.roll(total[2 * O :], SIZE - 1, 1))
    out[...] = (low + total[O : 2 * O] + high).T


def back_kernel(got, weight, out, grads):
    for row in range(H):
        for part in range(X):
            block = got[part, row, WT]
            pieces = [padded_slice(block, frame) for frame in range(WT)]
            for tap, source, target in own_taps():
                if source == row:
                    place = slice(target * COLS + part * W, target * COLS + (part + 1) * W)
                    for frame in range(WT):
                        grads[frame, place, tap * LANES : (tap + 1) * LANES] = pieces[frame]
    clear_borders(grads, LANES)
    operand = jnp.concatenate(
        [grads[tap : tap + T].reshape(SIZE, 3 * LANES) for tap in range(3)], axis=-1
    )
    total = jnp.dot(
        operand, weight[...].reshape(9 * LANES, 3 * C), preferred_element_type=F32
    )
    out[...] = shifted_sum([total[:, tap * C : (tap + 1) * C] for tap in range(3)])


INNER_ROWS = [(frame, row) for frame in range(T) for row in range(1, H - 1)]
OUTER_ROWS = [(frame, row) for frame in range(T) for row in (0, H - 1)]
BLOCKS = {place: block for block, place in enumerate(INNER_ROWS + OUTER_ROWS)}


def edge_kernel(up, down, ahead_weight, back_weight, ahead, back, out, data, grads):
    def put_back(frame, row, values):
        values = values.astype(BF16)
        for target in range(X):
            out[target, BLOCKS[frame, row]] = values[target * W : (target + 1) * W]

    def rows_of(values, frame, row):
        start = (frame * H + row) * COLS
        return values[start : start + COLS]

    for frame, row in INNER_ROWS:
        put_back(frame, row, rows_of(back, frame, row))
    ahead_parts, back_parts = [], []
    for side, rows in enumerate((up, down)):
        for part in range(X):
            place = slice(part * W, (part + 1) * W)
            for frame in range(WT):
                data[side, frame, place] = rows[part, frame]
                grads[side, frame, place] = padded_slice(rows[part, WT], frame)
        tap = 2 * side
        ahead_total = ahead_dot(
            jnp.concatenate(
                [data[side, time : time + T].reshape(T * COLS, C) for time in range(3)], axis=-1
            ),
            jnp.concatenate(
                [ahead_weight[time, :, tap * C : (tap + 1) * C] for time in range(3)], axis=-1
            ),
        )
        back_total = jnp.dot(
            jnp.concatenate(
                [grads[side, time : time + T].reshape(T * COLS, LANES) for time in range(3)],
                axis=-1,
            ),
            jnp.concatenate(
                [back_weight[time, tap * LANES : (tap + 1) * LANES] for time in range(3)], axis=0
            ),
            preferred_element_type=F32,
        )
        ahead_parts.append(shifted_sum([ahead_total[:, k * O : (k + 1) * O] for k in range(3)]))
        back_parts.append(shifted_sum([back_total[:, k * C : (k + 1) * C] for k in range(3)]))
    for frame, row in OUTER_ROWS:
        part = back_parts[row // (H - 1)][frame * COLS : (frame + 1) * COLS]
        put_back(frame, row, rows_of(back, frame, row) + part)
    for frame in range(T):
        rows = [rows_of(ahead, frame, row) for row in range(H)]
        for side, row in enumerate((0, H - 1)):
            rows[row] = rows[row] + ahead_parts[side][frame * COLS : (frame + 1) * COLS]
        rows = jnp.concatenate([row.astype(BF16) for row in rows], axis=-1)
        for target in range(X):
            out[target, T * H + frame] = rows[target * W : (target + 1) * W]


def arrived_grad(got, block):
    total = got[0, block].astype(F32)
    for source in range(1, X):
        total = total + got[source, block].astype(F32)
    return total


def arrived_conv(got, frame, row):
    return jnp.concatenate(
        [got[source, T * H + frame, :, row * O : (row + 1) * O] for source in range(X)], axis=-1
    ).astype(F32)


def middle_kernel(gains, got, active, grad_inner):
    scale = gains[1:2]
    for frame in range(T):
        for row in range(H):
            inner = arrived_conv(got, frame, row)
            grad_two = arrived_grad(got, BLOCKS[frame, row])
            normed, inverse = normalize(inner, scale)
            active[frame, row] = (normed * sigmoid(normed)).astype(BF16)
            grad_inner[frame, row] = norm_backward(
                inner, inverse, scale, grad_two * silu_slope(normed)
            ).astype(BF16)


def last_kernel(gains, latent, cotangent, got, block_out, latent_grad):
    scale = gains[0:1]
    for frame in range(T):
        for row in range(H):
            source = latent[frame, row].astype(F32)
            block_out[frame, row] = (source + arrived_conv(got, frame, row)).astype(BF16)
            normed, inverse = normalize(source, scale)
            grad_one = arrived_grad(got, BLOCKS[frame, row])
            latent_grad[frame, row] = (
                cotangent[frame, row].astype(F32)
                + norm_backward(source, inverse, scale, grad_one * silu_slope(normed))
            ).astype(BF16)


def shift(values, axis, by):
    size = lax.axis_size(axis)
    pairs = [(i, i + by) for i in range(size) if 0 <= i + by < size]
    return lax.ppermute(values, axis, pairs)


def exchange(values):
    return lax.all_to_all(values, "exp", split_axis=0, concat_axis=0, tiled=True)


def weights_kernel(ahead, back, ahead_out, back_out):
    zeros = jnp.zeros((LANES - O, 3 * C), BF16)
    for time_tap in range(3):
        for row_tap in range(3):
            start = row_tap * LANES
            for tap in range(3):
                ahead_out[
                    time_tap, tap * O : (tap + 1) * O, row_tap * C : (row_tap + 1) * C
                ] = ahead[time_tap, row_tap, tap]
                back_out[time_tap, start : start + O, tap * C : (tap + 1) * C] = back[
                    2 - time_tap, 2 - row_tap, 2 - tap
                ]
            back_out[time_tap, start + O : start + LANES] = zeros


WEIGHTS = [
    jax.ShapeDtypeStruct((3, 3 * O, 3 * C), BF16),
    jax.ShapeDtypeStruct((3, 3 * LANES, 3 * C), BF16),
]


def convs(packed, ahead, back):
    got = exchange(packed)
    ahead_weight, back_weight = call(weights_kernel, WEIGHTS, ahead, back)
    up = shift(got[:, H - 1], "seq", 1)
    down = shift(got[:, 0], "seq", -1)
    own_ahead = call(
        ahead_kernel,
        jax.ShapeDtypeStruct((SIZE, O), F32),
        got,
        ahead_weight,
        scratch=(pltpu.VMEM((WT, H * COLS, 3 * C), BF16),),
        flops=2 * SIZE * 27 * C * LANES,
    )
    own_back = call(
        back_kernel,
        jax.ShapeDtypeStruct((SIZE, C), F32),
        got,
        back_weight,
        scratch=(pltpu.VMEM((WT, H * COLS, 3 * LANES), BF16),),
        flops=2 * SIZE * 27 * C * LANES,
    )
    summed = jax.ShapeDtypeStruct((X, BACK, W, C), BF16)
    scratch = (pltpu.VMEM((2, WT, COLS, C), BF16), pltpu.VMEM((2, WT, COLS, LANES), BF16))
    summed = call(
        edge_kernel,
        summed,
        up,
        down,
        ahead_weight,
        back_weight,
        own_ahead,
        own_back,
        scratch=scratch,
        flops=SIZE * 9 * 2 * C * LANES,
    )
    return exchange(summed)


def body(latent, cotangent, gain_one, gain_two, kernel_one, kernel_two):
    gains = jnp.stack([gain_one, gain_two])
    block = jax.ShapeDtypeStruct((T, H, W, C), BF16)

    before = shift(latent, "section", 1)
    after = shift(cotangent, "section", -1)
    active, cot = call(
        own_kernel,
        [block, block],
        gains,
        latent,
        cotangent,
        scratch=(pltpu.VMEM((T, H, W, C), BF16), pltpu.SemaphoreType.DMA((2,))),
        far=2,
    )
    packed = pack(pack_kernel, gains, before, active, cot, after)
    got = convs(packed, kernel_one, kernel_two)
    active, grad_inner = call(middle_kernel, [block, block], gains, got)

    before = shift(active, "section", 1)
    after = shift(grad_inner, "section", -1)
    packed = pack(functools.partial(pack_kernel, None), before, active, grad_inner, after)
    got = convs(packed, kernel_two, kernel_one)
    return tuple(call(last_kernel, [block, block], gains, latent, cotangent, got))


def solution(mesh):
    in_specs = (
        P("section", "seq", "exp", None),
        P("section", "seq", "exp", None),
        P(),
        P(),
        P(None, None, None, "exp", None),
        P(None, None, None, "exp", None),
    )
    out_specs = (P("section", "seq", "exp", None), P("section", "seq", "exp", None))
    return jax.shard_map(body, mesh=mesh, in_specs=in_specs, out_specs=out_specs, check_vma=False)
```

```python
import functools
import jax
import jax.numpy as jnp
from jax import lax
from jax.experimental import pallas as pl
from jax.experimental.pallas import tpu as pltpu
from jax.sharding import PartitionSpec as P

epsilon = 1e-06
F32 = jnp.float32
BF16 = jnp.bfloat16

T, H, W, C, O, X = 2, 4, 16, 384, 96, 4
WT = T + 2
SIZE = T * H * W * X
COLS = X * W
LANES = 128
KINDS = WT + 1
BACK = T * H + T


def places(count, space):
    return [pl.BlockSpec(memory_space=space)] * count


def call(kernel, out_shape, *operands, scratch=(), flops=0, far=0, far_out=False):
    bytes_accessed = sum(a.size * a.dtype.itemsize for a in operands)
    outs = out_shape if isinstance(out_shape, (list, tuple)) else [out_shape]
    bytes_accessed += sum(a.size * a.dtype.itemsize for a in outs)
    near = len(operands) - far
    out_specs = places(len(outs), pltpu.VMEM) if outs is out_shape else places(1, pltpu.VMEM)[0]
    if far_out:
        out_shape = pltpu.HBM(out_shape.shape, out_shape.dtype)
        out_specs = pl.BlockSpec(memory_space=pltpu.HBM)
    pinned = [pltpu.with_memory_space_constraint(a, pltpu.HBM) for a in operands[near:]]
    return pl.pallas_call(
        kernel,
        out_shape=out_shape,
        in_specs=places(near, pltpu.VMEM) + places(far, pltpu.HBM),
        out_specs=out_specs,
        scratch_shapes=list(scratch),
        compiler_params=pltpu.CompilerParams(vmem_limit_bytes=40 * 1024 * 1024),
        cost_estimate=pl.CostEstimate(
            flops=flops, bytes_accessed=bytes_accessed, transcendentals=0
        ),
    )(*operands[:near], *pinned)


def sigmoid(values):
    return 1.0 / (1.0 + jnp.exp(-values))


def normalize(values, gain):
    inverse = lax.rsqrt(jnp.mean(values * values, axis=-1, keepdims=True) + epsilon)
    return values * inverse * gain, inverse


def norm_backward(values, inverse, gain, upstream):
    scaled = upstream * gain
    return inverse * scaled - values * inverse**3 * jnp.mean(
        values * scaled, axis=-1, keepdims=True
    )


def silu_slope(normed):
    sigma = sigmoid(normed)
    return sigma * (1.0 + normed * (1.0 - sigma))


def put_slices(out, row, blocks):
    for target in range(X):
        out[target, row, WT] = jnp.concatenate(
            [block[:, target * O : (target + 1) * O] for block in blocks], axis=-1
        )


def activated(block, scale):
    normed, _ = normalize(block.astype(F32), scale)
    return (normed * sigmoid(normed)).astype(BF16)


def put_block(out, row, frame, block):
    for target in range(X):
        out[target, row, frame] = block


def own_kernel(gains, own_far, cot_far, active, cot, own, sems):
    copies = [
        pltpu.make_async_copy(own_far, own, sems.at[0]),
        pltpu.make_async_copy(cot_far, cot, sems.at[1]),
    ]
    for copy in copies:
        copy.start()
    copies[0].wait()
    scale = gains[0:1]
    for row in range(H):
        for frame in range(T):
            active[frame, row] = activated(own[frame, row], scale)
    copies[1].wait()


def pack_kernel(gains, before, own, cot, after, out_far, out, sems):
    copies = []
    for row in range(H):
        for frame in range(T):
            block = before[frame, row]
            put_block(out, row, frame, block if gains is None else activated(block, gains[0:1]))
            put_block(out, row, T + frame, own[frame, row])
        put_slices(out, row, [cot[0, row], cot[1, row], after[0, row], after[1, row]])
        copies.append(pltpu.make_async_copy(out.at[:, row], out_far.at[:, row], sems.at[row]))
        copies[row].start()
    for copy in copies:
        copy.wait()


def pack(kernel, *operands):
    sent = jax.ShapeDtypeStruct((X, H, KINDS, W, C), BF16)
    scratch = (pltpu.VMEM(sent.shape, BF16), pltpu.SemaphoreType.DMA((H,)))
    return call(kernel, sent, *operands, scratch=scratch, far_out=True)


def shifted_sum(parts):
    size = parts[0].shape[0]
    column = lax.broadcasted_iota(jnp.int32, (size, 1), 0) % COLS
    low = jnp.where(column == 0, 0.0, pltpu.roll(parts[0], 1, 0))
    high = jnp.where(column == COLS - 1, 0.0, pltpu.roll(parts[2], size - 1, 0))
    return low + parts[1] + high


def ahead_dot(values, weight):
    return lax.dot_general(
        values, weight, (((1,), (1,)), ((), ())), preferred_element_type=F32
    )


def padded_slice(block, frame):
    zeros = jnp.zeros((W, LANES - O), BF16)
    return jnp.concatenate([block[:, frame * O : (frame + 1) * O], zeros], axis=-1)


OWN = {1: range(0, H), 2: range(2, H + 2)}
FLAGS = {1: {(0, 3): 0, (2, 4): 0}, 2: {(0, 0): 1, (2, 5): 0}}


def taps(phase, own):
    found = []
    for tap in range(3):
        for row in range(H + 2):
            target = row - tap
            if 0 <= target < H and (row in OWN[phase]) == own:
                flag = FLAGS[phase].get((tap, row)) if target in (0, 2, 3) else None
                found.append((tap, row, target, flag))
    return found


def masked(block, flags, flag):
    if flag is None:
        return block
    return block * flags[flag : flag + 1, : block.shape[1]].astype(BF16)


def clear_borders(operand, width, phase):
    given = [(tap, target) for tap, _, target, _ in taps(phase, True)]
    for tap in range(3):
        for row in range(H):
            if (tap, row) not in given:
                place = slice(row * COLS, (row + 1) * COLS)
                for frame in range(WT):
                    operand[frame, place, tap * width : (tap + 1) * width] = jnp.zeros(
                        (COLS, width), BF16
                    )


def ahead_kernel(phase, flags, got, weight, out, data):
    for tap, row, target, flag in taps(phase, True):
        for part in range(X):
            place = slice(target * COLS + part * W, target * COLS + (part + 1) * W)
            for frame in range(WT):
                block = masked(got[part, row - OWN[phase][0], frame], flags, flag)
                data[frame, place, tap * C : (tap + 1) * C] = block
    clear_borders(data, C, phase)
    total = jnp.zeros((3 * O, SIZE), F32)
    for time_tap in range(3):
        total = total + ahead_dot(
            weight[time_tap], data[time_tap : time_tap + T].reshape(SIZE, 3 * C)
        )
    column = lax.broadcasted_iota(jnp.int32, (1, SIZE), 1) % COLS
    low = jnp.where(column == 0, 0.0, pltpu.roll(total[:O], 1, 1))
    high = jnp.where(column == COLS - 1, 0.0, pltpu.roll(total[2 * O :], SIZE - 1, 1))
    out[...] = (low + total[O : 2 * O] + high).T


def back_kernel(phase, flags, got, weight, out, grads):
    for row in OWN[phase]:
        for part in range(X):
            block = got[part, row - OWN[phase][0], WT]
            pieces = [padded_slice(block, frame) for frame in range(WT)]
            for tap, source, target, flag in taps(phase, True):
                if source == row:
                    place = slice(target * COLS + part * W, target * COLS + (part + 1) * W)
                    for frame in range(WT):
                        piece = masked(pieces[frame], flags, flag)
                        grads[frame, place, tap * LANES : (tap + 1) * LANES] = piece
    clear_borders(grads, LANES, phase)
    operand = jnp.concatenate(
        [grads[tap : tap + T].reshape(SIZE, 3 * LANES) for tap in range(3)], axis=-1
    )
    total = jnp.dot(
        operand, weight[...].reshape(9 * LANES, 3 * C), preferred_element_type=F32
    )
    out[...] = shifted_sum([total[:, tap * C : (tap + 1) * C] for tap in range(3)])


def edge_kernel(
    phase, flags, rows, ahead_weight, back_weight, ahead, back, out, data, grads
):
    pairs = taps(phase, False)
    for number, (_, row, _, flag) in enumerate(pairs):
        near = row - (H if phase == 1 else 0)
        for part in range(X):
            place = slice(part * W, (part + 1) * W)
            for frame in range(WT):
                data[number, frame, place] = masked(rows[part, near, frame], flags, flag)
                piece = padded_slice(rows[part, near, WT], frame)
                grads[number, frame, place] = masked(piece, flags, flag)
    ahead_parts, back_parts = {}, {}
    for target in sorted({pair[2] for pair in pairs}):
        terms = [
            (number, pair[0], time)
            for number, pair in enumerate(pairs)
            if pair[2] == target
            for time in range(3)
        ]
        size = T * COLS
        total = ahead_dot(
            jnp.concatenate(
                [data[n, time : time + T].reshape(size, C) for n, _, time in terms], axis=-1
            ),
            jnp.concatenate(
                [ahead_weight[time, :, tap * C : (tap + 1) * C] for _, tap, time in terms], axis=-1
            ),
        )
        ahead_parts[target] = shifted_sum([total[:, k * O : (k + 1) * O] for k in range(3)])
        total = jnp.dot(
            jnp.concatenate(
                [grads[n, time : time + T].reshape(size, LANES) for n, _, time in terms], axis=-1
            ),
            jnp.concatenate(
                [back_weight[time, tap * LANES : (tap + 1) * LANES] for _, tap, time in terms],
                axis=0,
            ),
            preferred_element_type=F32,
        )
        back_parts[target] = shifted_sum([total[:, k * C : (k + 1) * C] for k in range(3)])
    for frame in range(T):
        packed = []
        for row in range(H):
            start = (frame * H + row) * COLS
            ahead_row, back_row = ahead[start : start + COLS], back[start : start + COLS]
            if row in ahead_parts:
                at = frame * COLS
                ahead_row = ahead_row + ahead_parts[row][at : at + COLS]
                back_row = back_row + back_parts[row][at : at + COLS]
            packed.append(ahead_row.astype(BF16))
            back_row = back_row.astype(BF16)
            for target in range(X):
                out[target, frame * H + row] = back_row[target * W : (target + 1) * W]
        packed = jnp.concatenate(packed, axis=-1)
        for target in range(X):
            out[target, T * H + frame] = packed[target * W : (target + 1) * W]


def arrived_grad(got, block):
    total = got[0, block].astype(F32)
    for source in range(1, X):
        total = total + got[source, block].astype(F32)
    return total


def arrived_conv(got, frame, row):
    return jnp.concatenate(
        [got[source, T * H + frame, :, row * O : (row + 1) * O] for source in range(X)], axis=-1
    ).astype(F32)


def middle_kernel(gains, got, active, grad_inner):
    scale = gains[1:2]
    for frame in range(T):
        for row in range(H):
            inner = arrived_conv(got, frame, row)
            grad_two = arrived_grad(got, frame * H + row)
            normed, inverse = normalize(inner, scale)
            active[frame, row] = (normed * sigmoid(normed)).astype(BF16)
            grad_inner[frame, row] = norm_backward(
                inner, inverse, scale, grad_two * silu_slope(normed)
            ).astype(BF16)


def last_kernel(gains, latent, cotangent, got, block_out, latent_grad):
    scale = gains[0:1]
    for frame in range(T):
        for row in range(H):
            source = latent[frame, row].astype(F32)
            block_out[frame, row] = (source + arrived_conv(got, frame, row)).astype(BF16)
            normed, inverse = normalize(source, scale)
            grad_one = arrived_grad(got, frame * H + row)
            latent_grad[frame, row] = (
                cotangent[frame, row].astype(F32)
                + norm_backward(source, inverse, scale, grad_one * silu_slope(normed))
            ).astype(BF16)


def shift(values, axis, by, wrap=False):
    size = lax.axis_size(axis)
    pairs = [(i, (i + by) % size) for i in range(size) if wrap or 0 <= i + by < size]
    return lax.ppermute(values, axis, pairs)


def exchange(values):
    return lax.all_to_all(values, "exp", split_axis=0, concat_axis=0, tiled=True)


def weights_kernel(ahead, back, ahead_out, back_out):
    zeros = jnp.zeros((LANES - O, 3 * C), BF16)
    for time_tap in range(3):
        for row_tap in range(3):
            start = row_tap * LANES
            for tap in range(3):
                ahead_out[
                    time_tap, tap * O : (tap + 1) * O, row_tap * C : (row_tap + 1) * C
                ] = ahead[time_tap, row_tap, tap]
                back_out[time_tap, start : start + O, tap * C : (tap + 1) * C] = back[
                    2 - time_tap, 2 - row_tap, 2 - tap
                ]
            back_out[time_tap, start + O : start + LANES] = zeros


WEIGHTS = [
    jax.ShapeDtypeStruct((3, 3 * O, 3 * C), BF16),
    jax.ShapeDtypeStruct((3, 3 * LANES, 3 * C), BF16),
]


def convs(phase, flags, packed, ahead, back):
    got = exchange(packed)
    ahead_weight, back_weight = call(weights_kernel, WEIGHTS, ahead, back)
    sent = got[:, :2] if phase == 1 else got[:, H - 2 :]
    rows = shift(sent, "seq", -1 if phase == 1 else 1, wrap=True)
    own_ahead = call(
        functools.partial(ahead_kernel, phase),
        jax.ShapeDtypeStruct((SIZE, O), F32),
        flags,
        got,
        ahead_weight,
        scratch=(pltpu.VMEM((WT, H * COLS, 3 * C), BF16),),
        flops=2 * SIZE * 27 * C * LANES,
    )
    own_back = call(
        functools.partial(back_kernel, phase),
        jax.ShapeDtypeStruct((SIZE, C), F32),
        flags,
        got,
        back_weight,
        scratch=(pltpu.VMEM((WT, H * COLS, 3 * LANES), BF16),),
        flops=2 * SIZE * 27 * C * LANES,
    )
    summed = jax.ShapeDtypeStruct((X, BACK, W, C), BF16)
    scratch = (pltpu.VMEM((3, WT, COLS, C), BF16), pltpu.VMEM((3, WT, COLS, LANES), BF16))
    summed = call(
        functools.partial(edge_kernel, phase),
        summed,
        flags,
        rows,
        ahead_weight,
        back_weight,
        own_ahead,
        own_back,
        scratch=scratch,
        flops=SIZE * 9 * 2 * C * LANES,
    )
    return exchange(summed)


def body(latent, cotangent, gain_one, gain_two, kernel_one, kernel_two):
    gains = jnp.stack([gain_one, gain_two])
    place = lax.axis_index("seq")
    flags = jnp.stack([place != lax.axis_size("seq") - 1, place != 0]).astype(F32)
    flags = jnp.broadcast_to(flags[:, None], (2, C))
    block = jax.ShapeDtypeStruct((T, H, W, C), BF16)

    before = shift(latent, "section", 1)
    after = shift(cotangent, "section", -1)
    active, cot = call(
        own_kernel,
        [block, block],
        gains,
        latent,
        cotangent,
        scratch=(pltpu.VMEM((T, H, W, C), BF16), pltpu.SemaphoreType.DMA((2,))),
        far=2,
    )
    packed = pack(pack_kernel, gains, before, active, cot, after)
    got = convs(1, flags, packed, kernel_one, kernel_two)
    active, grad_inner = call(middle_kernel, [block, block], gains, got)

    before = shift(active, "section", 1)
    after = shift(grad_inner, "section", -1)
    packed = pack(functools.partial(pack_kernel, None), before, active, grad_inner, after)
    got = convs(2, flags, packed, kernel_two, kernel_one)
    return tuple(call(last_kernel, [block, block], gains, latent, cotangent, got))


def solution(mesh):
    in_specs = (
        P("section", "seq", "exp", None),
        P("section", "seq", "exp", None),
        P(),
        P(),
        P(None, None, None, "exp", None),
        P(None, None, None, "exp", None),
    )
    out_specs = (P("section", "seq", "exp", None), P("section", "seq", "exp", None))
    return jax.shard_map(body, mesh=mesh, in_specs=in_specs, out_specs=out_specs, check_vma=False)
```
